32 devices in a mesh: groups: 2 (over x), out: 8 (over z, y), inp: 2 (over core).
Axes of the slice: x: 2, y: 2, z: 4, core: 2. Of those that a mesh axis runs over, the one named last changes fastest.
Arguments:
- pool: bfloat16 [8192, 5120], P('groups', 'out'), parts along dimension 0, may hold values from -6 to 6
- token_ids: int32 [384, 16], P(('groups', 'inp')), parts along dimension 0, may hold values from 0 to 4095
- weight: bfloat16 [5120, 27648], P('inp', 'out'), may hold values from -0.078125 to 0.078125
- factor_a: bfloat16 [384, 5120], P(('groups', 'inp'), 'out'), parts along dimension 0, may hold values from -6 to 6
- factor_b: bfloat16 [384, 27648], P(('groups', 'inp'), 'out'), parts along dimension 0, may hold values from -6 to 6
- ranks: int32 [384], P('groups'), parts along dimension 0, may hold values from 0 to 191, each once
Outputs:
- outputs: bfloat16 [6144, 27648], P(('groups', 'inp'), 'out'), parts along dimension 0
- direction: bfloat16 [10240, 27648], P(('groups', 'inp'), 'out'), parts along dimension 0
The draws below stay inside these ranges and needn't reach their ends.
There are 2 independent parts, one for each index of `groups`. The reference program is written for one: setup_inputs(seed, part) draws one part's arguments, and reference() takes and returns one part's arrays. A program takes and returns all parts, laid end to end along the dimension named above; an argument that names none is the same for every part. Nothing has to cross between parts.
Inputs may be any that keep to these rules, and one draw needn't show every extreme that they name: `ranks`: each of 0 to 191 once.
All inputs are finite; a program needn't handle non-finite values.
Results may differ from the reference program's by a relative error of at most 0.005.
Values may be sent and summed in bfloat16 or wider, within the bound.
A program may use at most 384 MiB of HBM per device.

```python
import math
import jax
import jax.numpy as jnp

D = 5120
F = 27648
SEQ = 16
POOL = 4096
MEMBERS = 192


def set_ends(drawn, own_key, low, top_value):
    longest = drawn.shape.index(max(drawn.shape))
    spots = []
    for shift in (0, 1):
        where = [jax.random.randint(jax.random.fold_in(own_key, axis), (), 0, length) for axis, length in enumerate(drawn.shape)]
        where[longest] = (where[longest] + shift) % drawn.shape[longest]
        spots.append(tuple(where))
    return drawn.at[spots[0]].set(low).at[spots[1]].set(top_value)


def level_of(own_key, shape, split, least, top_value):
    factor_of = 1.0
    for axis_at, blocks in split:
        draws = jax.random.uniform(jax.random.fold_in(jax.random.fold_in(own_key, 6), axis_at), (blocks,), jnp.float32, least / len(split), top_value / len(split))
        factor_of = factor_of * jnp.repeat(jnp.exp(draws), shape[axis_at] // blocks).reshape((-1,) + (1,) * (len(shape) - 1 - axis_at))
    return factor_of


def normal_values(rng, shape, width, most, pieces=(), dtype=jnp.bfloat16):
    array = jax.random.normal(rng, shape, jnp.float32) * width
    if len(pieces) > 0:
        array = level_of(rng, shape, pieces, -0.22, 0.18) * array
    return jnp.clip(array, min=-most, max=most).astype(dtype)


def setup_inputs(seed: int = 0, part: int = 0) -> dict:
    key_of = jax.random.split(jax.random.key(seed), 7)
    part_splits = jax.random.split(jax.random.fold_in(key_of[6], part), 7)
    return {
        "pool": normal_values(part_splits[0], (POOL, D), 1.0, 6.0, ((1, 8),)),
        "token_ids": set_ends(jax.random.randint(part_splits[1], (MEMBERS, SEQ), 0, POOL), jax.random.fold_in(part_splits[1], 1), 0, POOL - 1).astype(jnp.int32),
        "weight": normal_values(key_of[2], (D, F), D ** -0.5, 0.078125, ((0, 2), (1, 8))),
        "factor_a": normal_values(part_splits[3], (MEMBERS, D), 1.0, 6.0, ((0, 2), (1, 8))),
        "factor_b": normal_values(part_splits[4], (MEMBERS, F), 1.0, 6.0, ((0, 2), (1, 8))),
        "ranks": jax.random.permutation(part_splits[5], MEMBERS).astype(jnp.int32),
    }


def reference(pool, token_ids, weight, factor_a, factor_b, ranks):
    members = factor_a.shape[0]
    inputs = pool[token_ids.reshape(-1)]
    base = jnp.dot(inputs, weight, preferred_element_type=jnp.float32)
    reach = jnp.einsum('msd,md->ms', inputs.reshape(members, SEQ, D).astype(jnp.float32), factor_a.astype(jnp.float32))
    coef = 0.5 / math.sqrt(D)
    outputs = base.reshape(members, SEQ, F) + coef * reach[:, :, None] * factor_b.astype(jnp.float32)[:, None, :]
    outputs = outputs.reshape(members * SEQ, F).astype(jnp.bfloat16)
    shaping = 2.0 * ranks.astype(jnp.float32) / (members - 1) - 1.0
    scaled_b = (shaping[:, None] * factor_b.astype(jnp.float32) / math.sqrt(members)).astype(jnp.bfloat16)
    direction = jnp.dot(factor_a.T, scaled_b, preferred_element_type=jnp.float32).astype(jnp.bfloat16)
    return (outputs, direction)
```

```python
import functools
import math

import jax
import jax.numpy as jnp
from jax import lax
from jax.experimental import pallas as pl
from jax.experimental.pallas import tpu as pltpu
from jax.sharding import PartitionSpec as P

D = 5120
SEQ = 16
TILE = 256
F32 = jnp.float32
BF16 = jnp.bfloat16


def ring_order(n):
    if n <= 8:
        return list(range(0, n, 2)) + list(range(1, n, 2))[::-1]
    return list(range(n))


def block_kernel(n_blocks, has_acc, last, half_tiles, *refs):
    refs = list(refs[1:])
    tops = [refs.pop(0) for _ in range(n_blocks)]
    bottoms = [refs.pop(0) for _ in range(n_blocks)]
    weights = [refs.pop(0) for _ in range(n_blocks)]
    factors = [refs.pop(0) for _ in range(n_blocks)]
    acc_ref, reach_in = (refs.pop(0), refs.pop(0)) if has_acc else (None, None)
    b_ref = refs.pop(0) if last else None
    out_ref = refs.pop(0)
    reach_out = None if last else refs.pop(0)
    step = pl.program_id(0)

    def run(rows):
        reach = reach_in[...] if has_acc else None
        total = acc_ref[...] if has_acc else None
        for r_ref, w_ref, a_ref in zip(rows, weights, factors):
            r = r_ref[...]
            part = lax.dot_general(
                r, a_ref[...], (((1,), (1,)), ((), ())), preferred_element_type=F32
            )
            reach = part if reach is None else reach + part
            piece = jnp.dot(r, w_ref[...], preferred_element_type=F32)
            total = piece if total is None else total + piece
        if last:
            member = (lax.broadcasted_iota(jnp.int32, reach.shape, 0) + step * TILE) // SEQ
            own = lax.broadcasted_iota(jnp.int32, reach.shape, 1) == member
            scaled = jnp.where(own, reach * (0.5 / math.sqrt(D)), 0.0)
            high = scaled.astype(BF16)
            low = (scaled - high.astype(F32)).astype(BF16)
            total = total + jnp.dot(high, b_ref[...], preferred_element_type=F32)
            total = total + jnp.dot(low, b_ref[...], preferred_element_type=F32)
            out_ref[...] = total.astype(out_ref.dtype)
        else:
            out_ref[...] = total
            reach_out[...] = reach

    @pl.when(step < half_tiles)
    def _():
        run(tops)

    @pl.when(step >= half_tiles)
    def _():
        run(bottoms)


def add_blocks(owners, tops, bottoms, factors, weight, acc=None, factor_b=None):
    n_blocks = len(tops)
    half, width = tops[0].shape
    cols = weight.shape[1]
    members = factors[0].shape[0]
    half_tiles = half // TILE
    last = factor_b is not None
    rows = 2 * half

    def whole(shape):
        return pl.BlockSpec(shape, lambda i, own: (0, 0))

    def tile(width):
        return pl.BlockSpec((TILE, width), lambda i, own: (i, 0))

    specs = [
        pl.BlockSpec((TILE, width), lambda i, own: (jnp.minimum(i, half_tiles - 1), 0))
        for _ in tops
    ]
    specs += [
        pl.BlockSpec((TILE, width), lambda i, own: (jnp.maximum(i - half_tiles, 0), 0))
        for _ in bottoms
    ]
    specs += [
        pl.BlockSpec((width, cols), functools.partial(lambda k, i, own: (own[k], 0), k))
        for k in range(n_blocks)
    ]
    specs += [whole((members, width)) for _ in factors]
    operands = list(tops) + list(bottoms) + [weight] * n_blocks + list(factors)
    if acc is not None:
        specs += [tile(cols), tile(members)]
        operands += list(acc)
    if last:
        specs.append(whole((members, cols)))
        operands.append(factor_b)
        out_shape = jax.ShapeDtypeStruct((rows, cols), BF16)
        out_specs = tile(cols)
    else:
        out_shape = (
            jax.ShapeDtypeStruct((rows, cols), F32),
            jax.ShapeDtypeStruct((rows, members), F32),
        )
        out_specs = (tile(cols), tile(members))
    traffic = n_blocks * width * (rows + cols) * 2 + rows * cols * (
        (4 if acc is not None else 0) + (2 if last else 4)
    )
    return pl.pallas_call(
        functools.partial(block_kernel, n_blocks, acc is not None, last, half_tiles),
        grid_spec=pltpu.PrefetchScalarGridSpec(
            num_scalar_prefetch=1,
            grid=(rows // TILE,),
            in_specs=specs,
            out_specs=out_specs,
        ),
        out_shape=out_shape,
        cost_estimate=pl.CostEstimate(
            flops=2 * rows * width * cols * n_blocks, bytes_accessed=traffic, transcendentals=0
        ),
        compiler_params=pltpu.CompilerParams(vmem_limit_bytes=56 * 1024 * 1024),
    )(jnp.stack(owners).astype(jnp.int32), *operands)


def per_device(n, n_inp, pool, token_ids, weight, factor_a, factor_b, ranks):
    mem_local = factor_a.shape[0]
    members = ranks.shape[0]
    rows = mem_local * SEQ
    half = rows // 2
    width = pool.shape[1]
    inp_index = lax.axis_index("inp")
    me = lax.axis_index("out")

    order = ring_order(n)
    place = [order.index(j) for j in range(n)]
    up = [(order[k], order[(k + 1) % n]) for k in range(n)]
    down = [(order[(k + 1) % n], order[k]) for k in range(n)]
    order_of, place_of = jnp.array(order, jnp.int32), jnp.array(place, jnp.int32)

    def owner(shift):
        return order_of[(place_of[me] + shift + n) % n]

    def send(x, perm):
        return lax.ppermute(x, "out", perm)

    swap = [(0, 1), (1, 0)]

    a_of = {0: factor_a}
    for s in range(1, n // 2 + 1):
        a_of[-s] = send(a_of[-(s - 1)], up)
        if s < n // 2:
            a_of[s] = send(a_of[s - 1], down)
    b_other = lax.ppermute(factor_b, "inp", swap)

    ids = token_ids.reshape(-1)
    top, bottom = pool[ids[:half]], pool[ids[half:]]
    w_all = lax.all_gather(weight, "inp", axis=0, tiled=True)

    tops, bottoms = {0: top}, {0: bottom}
    for s in range(1, n // 2 + 1):
        tops[-s] = send(tops[-(s - 1)], up)
        bottoms[s] = send(bottoms[s - 1], down)
        if s < n // 2:
            tops[s] = send(tops[s - 1], down)
            bottoms[-s] = send(bottoms[-(s - 1)], up)
    bottoms[-(n // 2)] = bottoms[n // 2]

    a_all = jnp.zeros((n, mem_local, width), factor_a.dtype)
    for shift, block in a_of.items():
        a_all = lax.dynamic_update_slice(a_all, block[None], (owner(shift), 0, 0))
    per_half = n // n_inp

    def features(which):
        piece = lax.dynamic_slice_in_dim(a_all, which * per_half, per_half, 0)
        return piece.transpose(1, 0, 2).reshape(mem_local, per_half * width)

    a_own = features(inp_index)
    a_other = lax.ppermute(features(1 - inp_index), "inp", swap)
    shaping = 2.0 * ranks.astype(F32) / (members - 1) - 1.0
    norm_factor = 1.0 / math.sqrt(members)

    def scale(which, b):
        part = lax.dynamic_slice_in_dim(shaping, which * mem_local, mem_local, 0)
        return (part[:, None] * b.astype(F32) * norm_factor).astype(BF16)

    scaled = jnp.concatenate([scale(inp_index, factor_b), scale(1 - inp_index, b_other)], axis=0)
    a_pair = jnp.concatenate([a_own, a_other], axis=0)
    direction = lax.dot_general(
        a_pair, scaled, (((0,), (0,)), ((), ())), preferred_element_type=F32
    ).astype(BF16)

    def blocks(shifts, acc=None, b=None):
        return add_blocks(
            [owner(s) for s in shifts],
            [tops[s] for s in shifts],
            [bottoms[s] for s in shifts],
            [a_of[s] for s in shifts],
            w_all,
            acc,
            b,
        )

    acc = blocks([0, -1, 1])
    for s in range(2, n // 2):
        acc = blocks([-s, s], acc)
    outputs = blocks([-(n // 2)], acc, factor_b)
    return (outputs, direction)


def solution(mesh):
    placed = (
        P("groups", "out"),
        P(("groups", "inp"), None),
        P("inp", "out"),
        P(("groups", "inp"), "out"),
        P(("groups", "inp"), "out"),
        P("groups"),
    )
    return jax.shard_map(
        functools.partial(per_device, mesh.shape["out"], mesh.shape["inp"]),
        mesh=mesh,
        in_specs=placed,
        out_specs=(P(("groups", "inp"), "out"), P(("groups", "inp"), "out")),
        check_vma=False,
    )
```

```python
import functools
import math

import jax
import jax.numpy as jnp
from jax import lax
from jax.experimental import pallas as pl
from jax.experimental.pallas import tpu as pltpu
from jax.sharding import PartitionSpec as P

D = 5120
SEQ = 16
TILE = 256
F32 = jnp.float32
BF16 = jnp.bfloat16


def ring_order(n):
    if n <= 8:
        return list(range(0, n, 2)) + list(range(1, n, 2))[::-1]
    return list(range(n))


def block_kernel(n_blocks, has_acc, last, half_tiles, own_ref, *refs):
    refs = list(refs)
    tops = [refs.pop(0) for _ in range(n_blocks)]
    bottoms = [refs.pop(0) for _ in range(n_blocks)]
    factors = [refs.pop(0) for _ in range(n_blocks)]
    weight_ref = refs.pop(0)
    acc_ref, reach_in = (refs.pop(0), refs.pop(0)) if has_acc else (None, None)
    b_ref = refs.pop(0) if last else None
    out_ref = refs.pop(0)
    reach_out = None if last else refs.pop(0)
    held, sems = refs
    step = pl.program_id(0)
    width = tops[0].shape[1]
    members = factors[0].shape[0]

    @pl.when(step == 0)
    def _():
        copies = [
            pltpu.make_async_copy(
                weight_ref.at[pl.ds(pl.multiple_of(own_ref[k] * width, width), width)],
                held.at[pl.ds(k * width, width)],
                sems.at[k],
            )
            for k in range(n_blocks)
        ]
        for copy in copies:
            copy.start()
        if last:
            for k in range(2):
                held[pl.ds(n_blocks * width + k * members, members), :] = b_ref[...]
        for copy in copies:
            copy.wait()

    def run(rows):
        blocks = [r_ref[...] for r_ref in rows]
        reach = reach_in[...] if has_acc else None
        for r, a_ref in zip(blocks, factors):
            part = lax.dot_general(
                r, a_ref[...], (((1,), (1,)), ((), ())), preferred_element_type=F32
            )
            reach = part if reach is None else reach + part
        if last:
            member = (lax.broadcasted_iota(jnp.int32, reach.shape, 0) + step * TILE) // SEQ
            own = lax.broadcasted_iota(jnp.int32, reach.shape, 1) == member
            scaled = jnp.where(own, reach * (0.5 / math.sqrt(D)), 0.0)
            high = scaled.astype(BF16)
            low = (scaled - high.astype(F32)).astype(BF16)
            blocks += [high, low]
        left = blocks[0] if len(blocks) == 1 else jnp.concatenate(blocks, axis=1)
        total = jnp.dot(left, held[...], preferred_element_type=F32)
        if has_acc:
            total = total + acc_ref[...]
        out_ref[...] = total.astype(out_ref.dtype)
        if not last:
            reach_out[...] = reach

    @pl.when(step < half_tiles)
    def _():
        run(tops)

    @pl.when(step >= half_tiles)
    def _():
        run(bottoms)


def add_blocks(owners, tops, bottoms, factors, weight, acc=None, factor_b=None):
    n_blocks = len(tops)
    half, width = tops[0].shape
    cols = weight.shape[1]
    members = factors[0].shape[0]
    half_tiles = half // TILE
    last = factor_b is not None
    rows = 2 * half

    def whole(shape):
        return pl.BlockSpec(shape, lambda i, own: (0, 0))

    def tile(width):
        return pl.BlockSpec((TILE, width), lambda i, own: (i, 0))

    specs = [
        pl.BlockSpec((TILE, width), lambda i, own: (jnp.minimum(i, half_tiles - 1), 0))
        for _ in tops
    ]
    specs += [
        pl.BlockSpec((TILE, width), lambda i, own: (jnp.maximum(i - half_tiles, 0), 0))
        for _ in bottoms
    ]
    specs += [whole((members, width)) for _ in factors]
    specs.append(pl.BlockSpec(memory_space=pl.ANY))
    operands = list(tops) + list(bottoms) + list(factors) + [weight]
    if acc is not None:
        specs += [tile(cols), tile(members)]
        operands += list(acc)
    if last:
        specs.append(whole((members, cols)))
        operands.append(factor_b)
        out_shape = jax.ShapeDtypeStruct((rows, cols), BF16)
        out_specs = tile(cols)
    else:
        out_shape = (
            jax.ShapeDtypeStruct((rows, cols), F32),
            jax.ShapeDtypeStruct((rows, members), F32),
        )
        out_specs = (tile(cols), tile(members))
    depth = n_blocks * width + (2 * members if last else 0)
    traffic = n_blocks * width * (rows + cols) * 2 + rows * cols * (
        (4 if acc is not None else 0) + (2 if last else 4)
    )
    return pl.pallas_call(
        functools.partial(block_kernel, n_blocks, acc is not None, last, half_tiles),
        grid_spec=pltpu.PrefetchScalarGridSpec(
            num_scalar_prefetch=1,
            grid=(rows // TILE,),
            in_specs=specs,
            out_specs=out_specs,
            scratch_shapes=[
                pltpu.VMEM((depth, cols), BF16),
                pltpu.SemaphoreType.DMA((n_blocks,)),
            ],
        ),
        out_shape=out_shape,
        cost_estimate=pl.CostEstimate(
            flops=2 * rows * depth * cols, bytes_accessed=traffic, transcendentals=0
        ),
        compiler_params=pltpu.CompilerParams(vmem_limit_bytes=56 * 1024 * 1024),
    )(owners, *operands)


def per_device(n, n_inp, pool, token_ids, weight, factor_a, factor_b, ranks):
    mem_local = factor_a.shape[0]
    members = ranks.shape[0]
    rows = mem_local * SEQ
    half = rows // 2
    width = pool.shape[1]
    inp_index = lax.axis_index("inp")
    me = lax.axis_index("out")

    order = ring_order(n)
    place = [order.index(j) for j in range(n)]
    up = [(order[k], order[(k + 1) % n]) for k in range(n)]
    down = [(order[(k + 1) % n], order[k]) for k in range(n)]
    owners = [[order[(place[j] + s) % n] for s in range(-(n // 2), n // 2)] for j in range(n)]
    slots = [[row.index(j) for j in range(n)] for row in owners]
    table = lax.dynamic_index_in_dim(
        jnp.array([r + q for r, q in zip(owners, slots)], jnp.int32), me, 0, keepdims=False
    )

    def send(x, perm):
        return lax.ppermute(x, "out", perm)

    swap = [(0, 1), (1, 0)]

    lanes = -(-mem_local // 128) * 128
    pad = ((0, lanes - mem_local), (0, 0))
    a_of = {0: factor_a}
    for s in range(1, n // 2 + 1):
        a_of[-s] = send(a_of[-(s - 1)], up)
        if s < n // 2:
            a_of[s] = send(a_of[s - 1], down)
    b_other = lax.ppermute(factor_b, "inp", swap)

    ids = token_ids.reshape(-1)
    top, bottom = pool[ids[:half]], pool[ids[half:]]
    w_all = lax.all_gather(weight, "inp", axis=0, tiled=True)

    stacked = jnp.stack([a_of[s] for s in range(-(n // 2), n // 2)])
    per_half = n // n_inp

    def features(which):
        pieces = []
        mine = lax.dynamic_slice_in_dim(table, n + which * per_half, per_half)
        for k in range(per_half):
            pieces.append(lax.dynamic_index_in_dim(stacked, mine[k], 0, keepdims=False))
        return jnp.concatenate(pieces, axis=1)

    a_own = features(inp_index)
    a_other = lax.ppermute(features(1 - inp_index), "inp", swap)
    shaping = 2.0 * ranks.astype(F32) / (members - 1) - 1.0
    norm_factor = 1.0 / math.sqrt(members)

    def scale(which, b):
        part = lax.dynamic_slice_in_dim(shaping, which * mem_local, mem_local, 0)
        return (part[:, None] * b.astype(F32) * norm_factor).astype(BF16)

    scaled = jnp.concatenate([scale(inp_index, factor_b), scale(1 - inp_index, b_other)], axis=0)
    a_pair = jnp.concatenate([a_own, a_other], axis=0)
    direction = lax.dot_general(
        a_pair, scaled, (((0,), (0,)), ((), ())), preferred_element_type=F32
    ).astype(BF16)

    def blocks(shifts, acc=None, b=None):
        return add_blocks(
            jnp.concatenate([table[s + n // 2 : s + n // 2 + 1] for s in shifts]),
            [tops[s] for s in shifts],
            [bottoms[s] for s in shifts],
            [jnp.pad(a_of[s], pad) for s in shifts],
            w_all,
            acc,
            b,
        )

    tops, bottoms = {0: top}, {0: bottom}
    acc = None
    for s in range(1, n // 2 + 1):
        if s >= 3:
            acc = blocks([0, -1, 1]) if s == 3 else blocks([2 - s, s - 2], acc)
            ready = (tops[1 - s], tops[s - 1], bottoms[1 - s], bottoms[s - 1])
            ready, acc = lax.optimization_barrier((ready, acc))
            tops[1 - s], tops[s - 1], bottoms[1 - s], bottoms[s - 1] = ready
        tops[-s] = send(tops[-(s - 1)], up)
        bottoms[s] = send(bottoms[s - 1], down)
        if s < n // 2:
            tops[s] = send(tops[s - 1], down)
            bottoms[-s] = send(bottoms[-(s - 1)], up)
    bottoms[-(n // 2)] = bottoms[n // 2]
    acc = blocks([1 - n // 2, n // 2 - 1], acc)
    outputs = blocks([-(n // 2)], acc, jnp.pad(factor_b, pad))
    return (outputs, direction)


def solution(mesh):
    placed = (
        P("groups", "out"),
        P(("groups", "inp"), None),
        P("inp", "out"),
        P(("groups", "inp"), "out"),
        P(("groups", "inp"), "out"),
        P("groups"),
    )
    return jax.shard_map(
        functools.partial(per_device, mesh.shape["out"], mesh.shape["inp"]),
        mesh=mesh,
        in_specs=placed,
        out_specs=(P(("groups", "inp"), "out"), P(("groups", "inp"), "out")),
        check_vma=False,
    )
```

```python
import functools
import math

import jax
import jax.numpy as jnp
from jax import lax
from jax.experimental import pallas as pl
from jax.experimental.pallas import tpu as pltpu
from jax.sharding import PartitionSpec as P

D = 5120
SEQ = 16
TILE = 256
F32 = jnp.float32
BF16 = jnp.bfloat16


def ring_order(n):
    if n <= 8:
        return list(range(0, n, 2)) + list(range(1, n, 2))[::-1]
    return list(range(n))


def block_kernel(n_blocks, has_acc, last, half_tiles, own_ref, *refs):
    refs = list(refs)
    tops = [refs.pop(0) for _ in range(n_blocks)]
    bottoms = [refs.pop(0) for _ in range(n_blocks)]
    factors = [refs.pop(0) for _ in range(n_blocks)]
    weight_ref = refs.pop(0)
    acc_ref, reach_in = (refs.pop(0), refs.pop(0)) if has_acc else (None, None)
    b_ref = refs.pop(0) if last else None
    out_ref = refs.pop(0)
    reach_out = None if last else refs.pop(0)
    held, sems = refs
    step = pl.program_id(0)
    width = tops[0].shape[1]
    members = factors[0].shape[0]

    @pl.when(step == 0)
    def _():
        copies = [
            pltpu.make_async_copy(
                weight_ref.at[pl.ds(pl.multiple_of(own_ref[k] * width, width), width)],
                held.at[pl.ds(k * width, width)],
                sems.at[k],
            )
            for k in range(n_blocks)
        ]
        for copy in copies:
            copy.start()
        if last:
            for k in range(2):
                held[pl.ds(n_blocks * width + k * members, members), :] = b_ref[...]
        for copy in copies:
            copy.wait()

    def run(rows):
        blocks = [r_ref[...] for r_ref in rows]
        reach = reach_in[...] if has_acc else None
        for r, a_ref in zip(blocks, factors):
            part = lax.dot_general(
                r, a_ref[...], (((1,), (1,)), ((), ())), preferred_element_type=F32
            )
            reach = part if reach is None else reach + part
        if last:
            member = (lax.broadcasted_iota(jnp.int32, reach.shape, 0) + step * TILE) // SEQ
            own = lax.broadcasted_iota(jnp.int32, reach.shape, 1) == member
            scaled = jnp.where(own, reach * (0.5 / math.sqrt(D)), 0.0)
            high = scaled.astype(BF16)
            low = (scaled - high.astype(F32)).astype(BF16)
            blocks += [high, low]
        left = blocks[0] if len(blocks) == 1 else jnp.concatenate(blocks, axis=1)
        total = jnp.dot(left, held[...], preferred_element_type=F32)
        if has_acc:
            total = total + acc_ref[...]
        out_ref[...] = total.astype(out_ref.dtype)
        if not last:
            reach_out[...] = reach

    @pl.when(step < half_tiles)
    def _():
        run(tops)

    @pl.when(step >= half_tiles)
    def _():
        run(bottoms)


def add_blocks(owners, tops, bottoms, factors, weight, acc=None, factor_b=None):
    n_blocks = len(tops)
    half, width = tops[0].shape
    cols = weight.shape[1]
    members = factors[0].shape[0]
    half_tiles = half // TILE
    last = factor_b is not None
    rows = 2 * half

    def whole(shape):
        return pl.BlockSpec(shape, lambda i, own: (0, 0))

    def tile(width):
        return pl.BlockSpec((TILE, width), lambda i, own: (i, 0))

    specs = [
        pl.BlockSpec((TILE, width), lambda i, own: (jnp.minimum(i, half_tiles - 1), 0))
        for _ in tops
    ]
    specs += [
        pl.BlockSpec((TILE, width), lambda i, own: (jnp.maximum(i - half_tiles, 0), 0))
        for _ in bottoms
    ]
    specs += [whole((members, width)) for _ in factors]
    specs.append(pl.BlockSpec(memory_space=pl.ANY))
    operands = list(tops) + list(bottoms) + list(factors) + [weight]
    if acc is not None:
        specs += [tile(cols), tile(members)]
        operands += list(acc)
    if last:
        specs.append(whole((members, cols)))
        operands.append(factor_b)
        out_shape = jax.ShapeDtypeStruct((rows, cols), BF16)
        out_specs = tile(cols)
    else:
        out_shape = (
            jax.ShapeDtypeStruct((rows, cols), F32),
            jax.ShapeDtypeStruct((rows, members), F32),
        )
        out_specs = (tile(cols), tile(members))
    depth = n_blocks * width + (2 * members if last else 0)
    traffic = n_blocks * width * (rows + cols) * 2 + rows * cols * (
        (4 if acc is not None else 0) + (2 if last else 4)
    )
    return pl.pallas_call(
        functools.partial(block_kernel, n_blocks, acc is not None, last, half_tiles),
        grid_spec=pltpu.PrefetchScalarGridSpec(
            num_scalar_prefetch=1,
            grid=(rows // TILE,),
            in_specs=specs,
            out_specs=out_specs,
            scratch_shapes=[
                pltpu.VMEM((depth, cols), BF16),
                pltpu.SemaphoreType.DMA((n_blocks,)),
            ],
        ),
        out_shape=out_shape,
        cost_estimate=pl.CostEstimate(
            flops=2 * rows * depth * cols, bytes_accessed=traffic, transcendentals=0
        ),
        compiler_params=pltpu.CompilerParams(vmem_limit_bytes=56 * 1024 * 1024),
    )(owners, *operands)


def per_device(n, n_inp, pool, token_ids, weight, factor_a, factor_b, ranks):
    mem_local = factor_a.shape[0]
    members = ranks.shape[0]
    rows = mem_local * SEQ
    half = rows // 2
    width = pool.shape[1]
    inp_index = lax.axis_index("inp")
    me = lax.axis_index("out")

    order = ring_order(n)
    place = [order.index(j) for j in range(n)]
    up = [(order[k], order[(k + 1) % n]) for k in range(n)]
    down = [(order[(k + 1) % n], order[k]) for k in range(n)]
    owners = [[order[(place[j] + s) % n] for s in range(-(n // 2), n // 2)] for j in range(n)]
    slots = [[row.index(j) for j in range(n)] for row in owners]
    table = lax.dynamic_index_in_dim(
        jnp.array([r + q for r, q in zip(owners, slots)], jnp.int32), me, 0, keepdims=False
    )

    def send(x, perm):
        return lax.ppermute(x, "out", perm)

    swap = [(0, 1), (1, 0)]

    lanes = -(-mem_local // 128) * 128
    pad = ((0, lanes - mem_local), (0, 0))
    a_of = {0: factor_a}
    for s in range(-(n // 2), n // 2):
        if s != 0:
            a_of[s] = send(factor_a, [(order[(k + s) % n], order[k]) for k in range(n)])
    b_other = lax.ppermute(factor_b, "inp", swap)

    ids = token_ids.reshape(-1)
    top, bottom = pool[ids[:half]], pool[ids[half:]]
    w_all = lax.all_gather(weight, "inp", axis=0, tiled=True)

    stacked = jnp.stack([a_of[s] for s in range(-(n // 2), n // 2)])
    per_half = n // n_inp

    def features(which):
        pieces = []
        mine = lax.dynamic_slice_in_dim(table, n + which * per_half, per_half)
        for k in range(per_half):
            pieces.append(lax.dynamic_index_in_dim(stacked, mine[k], 0, keepdims=False))
        return jnp.concatenate(pieces, axis=1)

    a_own = features(inp_index)
    a_other = lax.ppermute(features(1 - inp_index), "inp", swap)
    shaping = 2.0 * ranks.astype(F32) / (members - 1) - 1.0
    norm_factor = 1.0 / math.sqrt(members)

    def scale(which, b):
        part = lax.dynamic_slice_in_dim(shaping, which * mem_local, mem_local, 0)
        return (part[:, None] * b.astype(F32) * norm_factor).astype(BF16)

    scaled = jnp.concatenate([scale(inp_index, factor_b), scale(1 - inp_index, b_other)], axis=0)
    a_pair = jnp.concatenate([a_own, a_other], axis=0)
    direction = lax.dot_general(
        a_pair, scaled, (((0,), (0,)), ((), ())), preferred_element_type=F32
    ).astype(BF16)

    def blocks(shifts, acc=None, b=None):
        return add_blocks(
            jnp.concatenate([table[s + n // 2 : s + n // 2 + 1] for s in shifts]),
            [tops[s] for s in shifts],
            [bottoms[s] for s in shifts],
            [jnp.pad(a_of[s], pad) for s in shifts],
            w_all,
            acc,
            b,
        )

    tops, bottoms = {0: top}, {0: bottom}
    acc = None
    for s in range(1, n // 2 + 1):
        if s >= 3:
            acc = blocks([0, -1, 1]) if s == 3 else blocks([2 - s, s - 2], acc)
            ready = (tops[1 - s], tops[s - 1], bottoms[1 - s], bottoms[s - 1])
            ready, acc = lax.optimization_barrier((ready, acc))
            tops[1 - s], tops[s - 1], bottoms[1 - s], bottoms[s - 1] = ready
        tops[-s] = send(tops[-(s - 1)], up)
        bottoms[s] = send(bottoms[s - 1], down)
        if s < n // 2:
            tops[s] = send(tops[s - 1], down)
            bottoms[-s] = send(bottoms[-(s - 1)], up)
    bottoms[-(n // 2)] = bottoms[n // 2]
    acc = blocks([1 - n // 2, n // 2 - 1], acc)
    outputs = blocks([-(n // 2)], acc, jnp.pad(factor_b, pad))
    return (outputs, direction)


def solution(mesh):
    placed = (
        P("groups", "out"),
        P(("groups", "inp"), None),
        P("inp", "out"),
        P(("groups", "inp"), "out"),
        P(("groups", "inp"), "out"),
        P("groups"),
    )
    return jax.shard_map(
        functools.partial(per_device, mesh.shape["out"], mesh.shape["inp"]),
        mesh=mesh,
        in_specs=placed,
        out_specs=(P(("groups", "inp"), "out"), P(("groups", "inp"), "out")),
        check_vma=False,
    )
```

```python
import functools
import math

import jax
import jax.numpy as jnp
from jax import lax
from jax.experimental import pallas as pl
from jax.experimental.pallas import tpu as pltpu
from jax.sharding import PartitionSpec as P

D = 5120
SEQ = 16
TILE = 256
F32 = jnp.float32
BF16 = jnp.bfloat16


def ring_order(n):
    if n <= 8:
        return list(range(0, n, 2)) + list(range(1, n, 2))[::-1]
    return list(range(n))


def block_kernel(n_blocks, has_acc, last, half_tiles, own_ref, *refs):
    refs = list(refs)
    tops = [refs.pop(0) for _ in range(n_blocks)]
    bottoms = [refs.pop(0) for _ in range(n_blocks)]
    factors = [refs.pop(0) for _ in range(n_blocks)]
    weight_ref = refs.pop(0)
    acc_ref, reach_in = (refs.pop(0), refs.pop(0)) if has_acc else (None, None)
    b_ref = refs.pop(0) if last else None
    out_ref = refs.pop(0)
    reach_out = None if last else refs.pop(0)
    held, sems = refs
    step = pl.program_id(0)
    width = tops[0].shape[1]
    members = factors[0].shape[0]

    @pl.when(step == 0)
    def _():
        copies = [
            pltpu.make_async_copy(
                weight_ref.at[pl.ds(pl.multiple_of(own_ref[k] * width, width), width)],
                held.at[pl.ds(k * width, width)],
                sems.at[k],
            )
            for k in range(n_blocks)
        ]
        for copy in copies:
            copy.start()
        if last:
            for k in range(2):
                held[pl.ds(n_blocks * width + k * members, members), :] = b_ref[...]
        for copy in copies:
            copy.wait()

    def run(rows):
        blocks = [r_ref[...] for r_ref in rows]
        reach = reach_in[...] if has_acc else None
        for r, a_ref in zip(blocks, factors):
            part = lax.dot_general(
                r, a_ref[...], (((1,), (1,)), ((), ())), preferred_element_type=F32
            )
            reach = part if reach is None else reach + part
        if last:
            member = (lax.broadcasted_iota(jnp.int32, reach.shape, 0) + step * TILE) // SEQ
            own = lax.broadcasted_iota(jnp.int32, reach.shape, 1) == member
            scaled = jnp.where(own, reach * (0.5 / math.sqrt(D)), 0.0)
            high = scaled.astype(BF16)
            low = (scaled - high.astype(F32)).astype(BF16)
            blocks += [high, low]
        left = blocks[0] if len(blocks) == 1 else jnp.concatenate(blocks, axis=1)
        total = jnp.dot(left, held[...], preferred_element_type=F32)
        if has_acc:
            total = total + acc_ref[...]
        out_ref[...] = total.astype(out_ref.dtype)
        if not last:
            reach_out[...] = reach

    @pl.when(step < half_tiles)
    def _():
        run(tops)

    @pl.when(step >= half_tiles)
    def _():
        run(bottoms)


def add_blocks(owners, tops, bottoms, factors, weight, acc=None, factor_b=None):
    n_blocks = len(tops)
    half, width = tops[0].shape
    cols = weight.shape[1]
    members = factors[0].shape[0]
    half_tiles = half // TILE
    last = factor_b is not None
    rows = 2 * half

    def whole(shape):
        return pl.BlockSpec(shape, lambda i, own: (0, 0))

    def tile(width):
        return pl.BlockSpec((TILE, width), lambda i, own: (i, 0))

    specs = [
        pl.BlockSpec((TILE, width), lambda i, own: (jnp.minimum(i, half_tiles - 1), 0))
        for _ in tops
    ]
    specs += [
        pl.BlockSpec((TILE, width), lambda i, own: (jnp.maximum(i - half_tiles, 0), 0))
        for _ in bottoms
    ]
    specs += [whole((members, width)) for _ in factors]
    specs.append(pl.BlockSpec(memory_space=pl.ANY))
    operands = list(tops) + list(bottoms) + list(factors) + [weight]
    if acc is not None:
        specs += [tile(cols), tile(members)]
        operands += list(acc)
    if last:
        specs.append(whole((members, cols)))
        operands.append(factor_b)
        out_shape = jax.ShapeDtypeStruct((rows, cols), BF16)
        out_specs = tile(cols)
    else:
        out_shape = (
            jax.ShapeDtypeStruct((rows, cols), F32),
            jax.ShapeDtypeStruct((rows, members), F32),
        )
        out_specs = (tile(cols), tile(members))
    depth = n_blocks * width + (2 * members if last else 0)
    traffic = n_blocks * width * (rows + cols) * 2 + rows * cols * (
        (4 if acc is not None else 0) + (2 if last else 4)
    )
    return pl.pallas_call(
        functools.partial(block_kernel, n_blocks, acc is not None, last, half_tiles),
        grid_spec=pltpu.PrefetchScalarGridSpec(
            num_scalar_prefetch=1,
            grid=(rows // TILE,),
            in_specs=specs,
            out_specs=out_specs,
            scratch_shapes=[
                pltpu.VMEM((depth, cols), BF16),
                pltpu.SemaphoreType.DMA((n_blocks,)),
            ],
        ),
        out_shape=out_shape,
        cost_estimate=pl.CostEstimate(
            flops=2 * rows * depth * cols, bytes_accessed=traffic, transcendentals=0
        ),
        compiler_params=pltpu.CompilerParams(vmem_limit_bytes=56 * 1024 * 1024),
    )(owners, *operands)


def per_device(n, n_inp, pool, token_ids, weight, factor_a, factor_b, ranks):
    mem_local = factor_a.shape[0]
    members = ranks.shape[0]
    rows = mem_local * SEQ
    half = rows // 2
    width = pool.shape[1]
    inp_index = lax.axis_index("inp")
    me = lax.axis_index("out")

    order = ring_order(n)
    place = [order.index(j) for j in range(n)]
    up = [(order[k], order[(k + 1) % n]) for k in range(n)]
    down = [(order[(k + 1) % n], order[k]) for k in range(n)]
    owners = [[order[(place[j] + s) % n] for s in range(-(n // 2), n // 2)] for j in range(n)]
    slots = [[row.index(j) for j in range(n)] for row in owners]
    table = lax.dynamic_index_in_dim(
        jnp.array([r + q for r, q in zip(owners, slots)], jnp.int32), me, 0, keepdims=False
    )

    def send(x, perm):
        return lax.ppermute(x, "out", perm)

    swap = [(0, 1), (1, 0)]

    b_other = lax.ppermute(factor_b, "inp", swap)

    ids = token_ids.reshape(-1)
    top, bottom = pool[ids[:half]], pool[ids[half:]]
    lanes = -(-mem_local // 128) * 128
    pad = ((0, lanes - mem_local), (0, 0))
    a_sent, top, bottom = lax.optimization_barrier((factor_a, top, bottom))
    a_of = {0: factor_a}
    for s in range(-(n // 2), n // 2):
        if s != 0:
            a_of[s] = send(a_sent, [(order[(k + s) % n], order[k]) for k in range(n)])
    w_all = lax.all_gather(weight, "inp", axis=0, tiled=True)

    stacked = jnp.stack([a_of[s] for s in range(-(n // 2), n // 2)])
    per_half = n // n_inp

    def features(which):
        pieces = []
        mine = lax.dynamic_slice_in_dim(table, n + which * per_half, per_half)
        for k in range(per_half):
            pieces.append(lax.dynamic_index_in_dim(stacked, mine[k], 0, keepdims=False))
        return jnp.concatenate(pieces, axis=1)

    a_own = features(inp_index)
    a_other = lax.ppermute(features(1 - inp_index), "inp", swap)
    shaping = 2.0 * ranks.astype(F32) / (members - 1) - 1.0
    norm_factor = 1.0 / math.sqrt(members)

    def scale(which, b):
        part = lax.dynamic_slice_in_dim(shaping, which * mem_local, mem_local, 0)
        return (part[:, None] * b.astype(F32) * norm_factor).astype(BF16)

    scaled = jnp.concatenate([scale(inp_index, factor_b), scale(1 - inp_index, b_other)], axis=0)
    a_pair = jnp.concatenate([a_own, a_other], axis=0)
    direction = lax.dot_general(
        a_pair, scaled, (((0,), (0,)), ((), ())), preferred_element_type=F32
    ).astype(BF16)

    def blocks(shifts, acc=None, b=None):
        return add_blocks(
            jnp.concatenate([table[s + n // 2 : s + n // 2 + 1] for s in shifts]),
            [tops[s] for s in shifts],
            [bottoms[s] for s in shifts],
            [jnp.pad(a_of[s], pad) for s in shifts],
            w_all,
            acc,
            b,
        )

    tops, bottoms = {0: top}, {0: bottom}
    acc = None
    for s in range(1, n // 2 + 1):
        if s >= 3:
            acc = blocks([0, -1, 1]) if s == 3 else blocks([2 - s, s - 2], acc)
            ready = (tops[1 - s], tops[s - 1], bottoms[1 - s], bottoms[s - 1])
            ready, acc = lax.optimization_barrier((ready, acc))
            tops[1 - s], tops[s - 1], bottoms[1 - s], bottoms[s - 1] = ready
        tops[-s] = send(tops[-(s - 1)], up)
        bottoms[s] = send(bottoms[s - 1], down)
        if s < n // 2:
            tops[s] = send(tops[s - 1], down)
            bottoms[-s] = send(bottoms[-(s - 1)], up)
    bottoms[-(n // 2)] = bottoms[n // 2]
    acc = blocks([1 - n // 2, n // 2 - 1], acc)
    outputs = blocks([-(n // 2)], acc, jnp.pad(factor_b, pad))
    return (outputs, direction)


def solution(mesh):
    placed = (
        P("groups", "out"),
        P(("groups", "inp"), None),
        P("inp", "out"),
        P(("groups", "inp"), "out"),
        P(("groups", "inp"), "out"),
        P("groups"),
    )
    return jax.shard_map(
        functools.partial(per_device, mesh.shape["out"], mesh.shape["inp"]),
        mesh=mesh,
        in_specs=placed,
        out_specs=(P(("groups", "inp"), "out"), P(("groups", "inp"), "out")),
        check_vma=False,
    )
```
